128 devices in a mesh: ctx: 8 (over y, z_hi), rep: 16 (over x, z_lo, core).
Axes of the slice: x: 4, y: 4, z: 4 (z_hi: 2, z_lo: 2; z = z_hi * 2 + z_lo), core: 2. Of those that a mesh axis runs over, the one named last changes fastest.
Arguments:
- queries: bfloat16 [16, 4096, 8192], P('rep', 'ctx'), may hold values from -20 to 20
- keys: bfloat16 [16, 4096, 1024], P('rep', 'ctx'), may hold values from -20 to 20
- values: bfloat16 [16, 4096, 1024], P('rep', 'ctx'), may hold values from -6 to 6
- doc_lengths: int32 [16, 16], replicated, may hold values from 1 to 1024, 4096 in all within a row
Outputs:
- attended: bfloat16 [16, 4096, 8192], P('rep', 'ctx')
The draws below stay inside these ranges and needn't reach their ends.
All inputs are finite; a program needn't handle non-finite values.
Results may differ from the reference program's by a relative error of at most 0.0075.
Values may be sent and summed in bfloat16 or wider, within the bound.
A program may use at most 192 MiB of HBM per device.

```python
import math
import jax
import jax.numpy as jnp
import numpy as np
from jax import lax

HQ = 64
KEY_HEADS = 8
HEAD_SIZE = 128
S_DEV = 512
NDOC = 16
QUERY_PER_KEY = 8
PACKED_LENGTH = 4096
PACKED_COUNT = 16
N_CTX = 8


def drawn_plan(key):
    common_span = jnp.clip(jax.random.normal(jax.random.fold_in(key, 7), (PACKED_COUNT, PACKED_LENGTH, KEY_HEADS * HEAD_SIZE), jnp.float32), -4.0, 4.0)
    return common_span


def draw_keys(key, part):
    common_span = drawn_plan(key)
    result = common_span
    return result.astype(jnp.bfloat16)


def draw_queries(key, part):
    drawn = jnp.clip(jax.random.normal(jax.random.fold_in(key, 3), (PACKED_COUNT, PACKED_LENGTH, HQ * HEAD_SIZE), jnp.float32), -4.0, 4.0)
    return drawn.astype(jnp.bfloat16)


def shard_levels(stream_key, shape, split, smallest, top_value):
    factor_of = 1.0
    for position, blocks in split:
        heights = jax.random.uniform(jax.random.fold_in(jax.random.fold_in(stream_key, 6), position), (blocks,), jnp.float32, smallest / len(split), top_value / len(split))
        factor_of = factor_of * jnp.repeat(jnp.exp(heights), shape[position] // blocks).reshape((-1,) + (1,) * (len(shape) - 1 - position))
    return factor_of


def profile(number_of, total, limit, skew):
    portions = [(1 << 20) // math.isqrt(standing ** skew) + 1 for standing in range(2, number_of + 1)]
    spare, given = total - limit - (number_of - 1), [1] * (number_of - 1)
    while spare > 0:
        candidates = [i for i in range(number_of - 1) if given[i] < limit]
        pool, remaining = sum([portions[i] for i in candidates]), spare
        for i in candidates:
            extra = min(limit - given[i], max(1, remaining * portions[i] // pool), spare)
            given[i] = given[i] + extra
            spare = spare - extra
    return np.array([limit] + given)


def ragged(rng, number_of, total, reach, skew):
    if number_of == 2:
        one = jax.random.randint(rng, (), max(1, total - reach), min(reach, total - 1) + 1)
        return jnp.stack([one, total - one])
    lengths = jnp.asarray(profile(number_of, total, reach, skew), jnp.int32)
    twos = (number_of - 1) // 2
    donor, receiver = lengths[1:1 + 2 * twos:2], lengths[2:2 + 2 * twos:2]
    slack = jnp.minimum(donor - 1, reach - receiver)
    passed = jax.random.randint(jax.random.fold_in(rng, 1), (twos,), 0, 1 << 20) % (slack + 1)
    lengths = lengths.at[1:1 + 2 * twos:2].set(donor - passed).at[2:2 + 2 * twos:2].set(receiver + passed)
    return lengths[jax.random.permutation(jax.random.fold_in(rng, 2), number_of)]


def bell_draw(key, shape, width, limit, pieces=(), held_as=jnp.bfloat16):
    values = width * jax.random.normal(key, shape, jnp.float32)
    if pieces:
        values = values * shard_levels(key, shape, pieces, -0.22, 0.18)
    return jnp.clip(values, -limit, limit).astype(held_as)


def setup_inputs(seed: int = 0) -> dict:
    splits = jax.random.split(jax.random.key(seed), 5)
    queries = draw_queries(jax.random.fold_in(splits[4], 71), 0)
    keys = draw_keys(jax.random.fold_in(splits[4], 71), 0)
    values = bell_draw(splits[2], (PACKED_COUNT, PACKED_LENGTH, KEY_HEADS * HEAD_SIZE), 1.0, 6.0, ((0, 16), (1, 8)))
    doc_lengths = jax.vmap(lambda own: ragged(own, NDOC, PACKED_LENGTH, PACKED_LENGTH // 4, 2))(jax.random.split(splits[3], PACKED_COUNT)).reshape((PACKED_COUNT, NDOC)).astype(jnp.int32)
    return dict(queries=queries, keys=keys, values=values, doc_lengths=doc_lengths)


def reference(queries, keys, values, doc_lengths):
    doc_ends = jnp.cumsum(doc_lengths, axis=1)
    positions = jnp.arange(PACKED_LENGTH, dtype=jnp.int32)
    segments = jnp.sum((positions[None, :, None] >= doc_ends[:, None, :]).astype(jnp.int32), axis=2)
    scale = HEAD_SIZE ** -0.5
    rows_per_block = S_DEV // 2
    visible_window = rows_per_block + PACKED_LENGTH // 4

    def one_replica(inputs):
        query_rows, rows_of_key, rows_of_value, segment_row = inputs

        def one_block(block):
            start = (block * rows_per_block).astype(jnp.int32)
            key_first_row = jnp.maximum(start + rows_per_block - visible_window, 0).astype(jnp.int32)
            query_tile_rows = lax.dynamic_slice_in_dim(query_rows, start, rows_per_block, 0)
            query_tile_rows = query_tile_rows.reshape(rows_per_block, KEY_HEADS, QUERY_PER_KEY, HEAD_SIZE).astype(jnp.float32)
            heads_of_key = lax.dynamic_slice_in_dim(rows_of_key, key_first_row, visible_window, 0).reshape(visible_window, KEY_HEADS, HEAD_SIZE).astype(jnp.float32)
            heads_of_value = lax.dynamic_slice_in_dim(rows_of_value, key_first_row, visible_window, 0).reshape(visible_window, KEY_HEADS, HEAD_SIZE).astype(jnp.float32)
            query_positions = start + jnp.arange(rows_per_block, dtype=jnp.int32)
            key_positions = key_first_row + jnp.arange(visible_window, dtype=jnp.int32)
            query_segment = lax.dynamic_slice_in_dim(segment_row, start, rows_per_block, 0)
            key_segment = lax.dynamic_slice_in_dim(segment_row, key_first_row, visible_window, 0)
            mask = (key_positions[None, :] <= query_positions[:, None]) & (key_segment[None, :] == query_segment[:, None])
            scores = jnp.einsum("qhgd,khd->hgqk", query_tile_rows, heads_of_key) * scale
            scores = jnp.where(mask[None, None], scores, -1e30)
            top = jnp.max(scores, axis=-1)
            weights = jnp.where(mask[None, None], jnp.exp(scores - top[..., None]), 0.0)
            total = jnp.sum(weights, axis=-1)
            rounded = lax.optimization_barrier(weights.astype(jnp.bfloat16)).astype(jnp.float32)
            output = jnp.einsum("hgqk,khd->hgqd", rounded, heads_of_value) / total[..., None]
            output = jnp.transpose(output, (2, 0, 1, 3)).reshape(rows_per_block, HQ * HEAD_SIZE)
            return output.astype(jnp.bfloat16)

        blocks = lax.map(one_block, jnp.arange(2 * N_CTX, dtype=jnp.int32))
        return blocks.reshape(PACKED_LENGTH, HQ * HEAD_SIZE)

    return lax.map(one_replica, (queries, keys, values, segments))
```

```python
import math

import jax
import jax.numpy as jnp
from jax import lax
from jax.experimental import pallas as pl
from jax.experimental.pallas import tpu as pltpu
from jax.sharding import PartitionSpec as P

MESH = pl.DeviceIdType.MESH
HQ = 64
KEY_HEADS = 8
HEAD_SIZE = 128
GROUP = 8
WIDTH = GROUP * HEAD_SIZE
ROWS = 512
TQ = 256
SPAN = 1280
SCALE = math.log2(math.e) / math.sqrt(HEAD_SIZE)
PER_STEP = 4
AHEAD = 3


def tile(t, q_ref, o_ref, kw, vw, bias):
    base = pl.multiple_of(t * TQ, TQ)

    def heads(i, carry):
        for j in range(PER_STEP):
            columns = pl.ds(pl.multiple_of((i * PER_STEP + j) * HEAD_SIZE, HEAD_SIZE), HEAD_SIZE)
            scores = lax.dot_general(
                q_ref[0, :, columns],
                kw[pl.ds(base, SPAN), :],
                (((1,), (1,)), ((), ())),
                preferred_element_type=jnp.float32,
            )
            scores = scores * SCALE + bias[t]
            top = jnp.max(scores, axis=1, keepdims=True)
            weights = jnp.exp2(scores - top).astype(jnp.bfloat16)
            out = jnp.dot(weights, vw[pl.ds(base, SPAN), :], preferred_element_type=jnp.float32)
            o_ref[0, :, columns] = (out[:, :HEAD_SIZE] / out[:, HEAD_SIZE:]).astype(jnp.bfloat16)
        return carry

    lax.fori_loop(0, GROUP // PER_STEP, heads, 0)


def kernel(
    q_ref, own_k, own_v, all_k, all_v, first_ref, o_ref,
    far_k, far_v, near_k, near_v, kw, vw, bias, send, recv,
):
    g = pl.program_id(0)
    t = pl.program_id(1)
    ctx = lax.axis_index("ctx")
    n = lax.axis_size("ctx")
    odd = lax.rem(ctx, 2)
    after = lax.rem(ctx + 2, n)
    before = lax.rem(ctx + n - 2, n)
    beside = ctx + 1 - 2 * odd

    def move(kind, h, source, target, device):
        return pltpu.make_async_remote_copy(
            src_ref=source,
            dst_ref=target.at[h],
            send_sem=send.at[kind, h],
            recv_sem=recv.at[kind, h],
            device_id={"ctx": device},
            device_id_type=MESH,
        )

    def own(ref, h):
        return ref.at[0, :, pl.ds(pl.multiple_of(h * HEAD_SIZE, HEAD_SIZE), HEAD_SIZE)]

    def far(h):
        return (
            move(0, h, own(all_k, h), far_k, after),
            move(1, h, own(all_v, h), far_v, after),
        )

    def near(h):
        return (
            move(2, h, own(all_k, h), near_k, beside),
            move(3, h, own(all_v, h), near_v, beside),
        )

    def relay(h):
        return (
            move(2, h, far_k.at[h], near_k, beside),
            move(3, h, far_v.at[h], near_v, beside),
        )

    def issue(h):
        for copy in far(h):
            copy.start()

        @pl.when(odd == 0)
        def _():
            for copy in near(h):
                copy.start()

    def forward(h):
        for copy in far(h):
            copy.wait_recv()

        @pl.when(odd == 1)
        def _():
            for copy in relay(h):
                copy.start()

    @pl.when((g == 0) & (t == 0))
    def _():
        barrier = pltpu.get_barrier_semaphore()
        for device in (after, before, beside):
            pl.semaphore_signal(barrier, inc=1, device_id={"ctx": device}, device_id_type=MESH)
        pl.semaphore_wait(barrier, 3)
        lax.fori_loop(0, AHEAD, lambda h, c: (issue(h), c)[1], 0)
        vw[:, HEAD_SIZE:] = jnp.ones((3 * ROWS, HEAD_SIZE), jnp.bfloat16)
        for i in range(2):
            column = i * TQ + lax.broadcasted_iota(jnp.int32, (TQ, SPAN), 1)
            row = 2 * ROWS + i * TQ + lax.broadcasted_iota(jnp.int32, (TQ, SPAN), 0)
            first = first_ref[i * TQ : (i + 1) * TQ, :]
            bias[i] = jnp.where((column >= first) & (column <= row), 0.0, -1e30)
        forward(0)

    @pl.when(t == 0)
    def _():
        @pl.when(g + AHEAD < KEY_HEADS)
        def _():
            issue(g + AHEAD)

        for copy in near(g):
            copy.wait_recv()
        kw[:ROWS, :] = far_k[g]
        vw[:ROWS, :HEAD_SIZE] = far_v[g]
        kw[ROWS : 2 * ROWS, :] = near_k[g]
        vw[ROWS : 2 * ROWS, :HEAD_SIZE] = near_v[g]
        kw[2 * ROWS :, :] = own_k[0]
        vw[2 * ROWS :, :HEAD_SIZE] = own_v[0]

    @pl.when((t == 1) & (g + 1 < KEY_HEADS))
    def _():
        forward(g + 1)

    tile(t, q_ref, o_ref, kw, vw, bias)

    @pl.when((g == KEY_HEADS - 1) & (t == 1))
    def _():
        def finish(h, carry):
            for copy in (*far(h), *near(h)):
                copy.wait_send()
            return carry

        lax.fori_loop(0, KEY_HEADS, finish, 0)


def attend(first, queries, keys, values):
    def own(g, t):
        return (0, 0, g)

    return pl.pallas_call(
        kernel,
        grid=(KEY_HEADS, ROWS // TQ),
        in_specs=[
            pl.BlockSpec((1, TQ, WIDTH), lambda g, t: (0, t, g)),
            pl.BlockSpec((1, ROWS, HEAD_SIZE), own),
            pl.BlockSpec((1, ROWS, HEAD_SIZE), own),
            pl.BlockSpec(memory_space=pl.ANY),
            pl.BlockSpec(memory_space=pl.ANY),
            pl.BlockSpec((ROWS, 1), lambda g, t: (0, 0)),
        ],
        out_specs=pl.BlockSpec((1, TQ, WIDTH), lambda g, t: (0, t, g)),
        scratch_shapes=[
            *[pltpu.VMEM((KEY_HEADS, ROWS, HEAD_SIZE), jnp.bfloat16)] * 4,
            pltpu.VMEM((3 * ROWS, HEAD_SIZE), jnp.bfloat16),
            pltpu.VMEM((3 * ROWS, 2 * HEAD_SIZE), jnp.bfloat16),
            pltpu.VMEM((2, TQ, SPAN), jnp.float32),
            pltpu.SemaphoreType.DMA((4, KEY_HEADS)),
            pltpu.SemaphoreType.DMA((4, KEY_HEADS)),
        ],
        out_shape=jax.ShapeDtypeStruct((1, ROWS, HQ * HEAD_SIZE), jnp.bfloat16),
        compiler_params=pltpu.CompilerParams(
            vmem_limit_bytes=50 << 20, collective_id=0, has_side_effects=True
        ),
    )(queries, keys, values, keys, values, first)


def on_device(queries, keys, values, doc_lengths):
    rep = lax.axis_index("rep")
    ctx = lax.axis_index("ctx")
    lengths = lax.dynamic_index_in_dim(doc_lengths, rep, 0, keepdims=False)
    order = jnp.arange(lengths.shape[0])
    starts = jnp.sum(jnp.where(order[None, :] < order[:, None], lengths[None, :], 0), axis=1)
    positions = ctx * ROWS + jnp.arange(ROWS, dtype=jnp.int32)
    first = jnp.max(jnp.where(starts[None, :] <= positions[:, None], starts[None, :], 0), axis=1)
    first = (first - (ctx - 2) * ROWS).astype(jnp.int32)
    return attend(first[:, None], queries, keys, values)


def solution(mesh):
    return jax.shard_map(
        on_device,
        mesh=mesh,
        in_specs=(P("rep", "ctx", None), P("rep", "ctx", None), P("rep", "ctx", None), P()),
        out_specs=P("rep", "ctx", None),
        check_vma=False,
    )
```

```python
import math

import jax
import jax.numpy as jnp
from jax import lax
from jax.experimental import pallas as pl
from jax.experimental.pallas import tpu as pltpu
from jax.sharding import PartitionSpec as P

MESH = pl.DeviceIdType.MESH
HQ = 64
KEY_HEADS = 8
HEAD_SIZE = 128
GROUP = 8
WIDTH = GROUP * HEAD_SIZE
ROWS = 512
TQ = 256
SPAN = 1280
SCALE = math.log2(math.e) / math.sqrt(HEAD_SIZE)
AHEAD = 3
PIECE = 128
PIECES = TQ // PIECE
TILES = SPAN // TQ
SLOTS = 4
LAG = 2
STEPS = 2 * KEY_HEADS
FAR_BELOW = -131072.0


def kernel(
    q_ref, q_extra, own_k, own_v, all_k, all_v, k_extra, o_ref,
    far_k, far_v, near_k, near_v, kw, vt, corner, scores, weights, tops, outs, send, recv, sent,
):
    s = pl.program_id(0)
    g = s // 2
    t = lax.rem(s, 2)
    ctx = lax.axis_index("ctx")
    n = lax.axis_size("ctx")
    odd = lax.rem(ctx, 2)
    after = lax.rem(ctx + 2, n)
    before = lax.rem(ctx + n - 2, n)
    beside = ctx + 1 - 2 * odd

    def move(kind, h, source, target, device):
        return pltpu.make_async_remote_copy(
            src_ref=source,
            dst_ref=target.at[h],
            send_sem=send.at[kind, h],
            recv_sem=recv.at[kind, h],
            device_id={"ctx": device},
            device_id_type=MESH,
        )

    def own(ref, h):
        return ref.at[0, :, pl.ds(pl.multiple_of(h * HEAD_SIZE, HEAD_SIZE), HEAD_SIZE)]

    def far(h):
        return (
            move(0, h, own(all_k, h), far_k, after),
            move(1, h, own(all_v, h), far_v, after),
        )

    def near(h):
        return (
            move(2, h, own(all_k, h), near_k, beside),
            move(3, h, own(all_v, h), near_v, beside),
        )

    def relay(h):
        return (
            move(2, h, far_k.at[h], near_k, beside),
            move(3, h, far_v.at[h], near_v, beside),
        )

    def issue(h):
        for copy in far(h):
            copy.start()

        @pl.when(odd == 0)
        def _():
            for copy in near(h):
                copy.start()

    def forward(h):
        for copy in far(h):
            copy.wait_recv()

        @pl.when(odd == 1)
        def _():
            for copy in relay(h):
                copy.start()

    def result(step):
        row = pl.multiple_of(lax.rem(step, 2) * TQ, TQ)
        column = pl.multiple_of(step // 2 * WIDTH, WIDTH)
        slot = lax.rem(step, 3)
        return pltpu.make_async_copy(
            outs.at[slot],
            o_ref.at[0, pl.ds(row, TQ), pl.ds(column, WIDTH)],
            sent.at[slot],
        )

    @pl.when(s == 0)
    def _():
        barrier = pltpu.get_barrier_semaphore()
        for device in (after, before, beside):
            pl.semaphore_signal(barrier, inc=1, device_id={"ctx": device}, device_id_type=MESH)
        pl.semaphore_wait(barrier, 3)
        lax.fori_loop(0, AHEAD, lambda h, c: (issue(h), c)[1], 0)
        kw[:, HEAD_SIZE:] = k_extra[...]
        for i in range(2):
            vt[i, HEAD_SIZE:, :] = jnp.ones((16, 3 * ROWS), jnp.bfloat16)
        below = lax.broadcasted_iota(jnp.int32, (TQ, TQ), 0)
        across = lax.broadcasted_iota(jnp.int32, (TQ, TQ), 1)
        corner[...] = jnp.where(below <= across, 0.0, FAR_BELOW)
        scores[2:] = jnp.zeros((2, SPAN, TQ), jnp.float32)
        tops[...] = jnp.zeros_like(tops)
        forward(0)

    @pl.when((t == 0) & (g < KEY_HEADS))
    def _():
        @pl.when(g + AHEAD < KEY_HEADS)
        def _():
            issue(g + AHEAD)

        for copy in near(g):
            copy.wait_recv()
        slot = lax.rem(g, 2)
        for i, (key, value) in enumerate(
            ((far_k[g], far_v[g]), (near_k[g], near_v[g]), (own_k[0], own_v[0]))
        ):
            kw[i * ROWS : (i + 1) * ROWS, :HEAD_SIZE] = key
            vt[slot, :HEAD_SIZE, i * ROWS : (i + 1) * ROWS] = value.T

    @pl.when((t == 1) & (g + 1 < KEY_HEADS))
    def _():
        forward(g + 1)

    @pl.when(s >= 3)
    def _():
        result(s - 3).wait()

    def work(acc, total):
        def columns(h):
            return slice(h * HEAD_SIZE, (h + 1) * HEAD_SIZE)

        base = pl.multiple_of(t * TQ, TQ)

        def score(h, unit, j, c):
            staged = None
            if j == 0 and c == 0:
                staged = 0
                query = jnp.concatenate([q_ref[0, :, columns(h)], q_extra[...]], axis=1)
                pltpu.matmul_push_rhs(query, 0, unit, transpose=True)
            pltpu.matmul_acc_lhs(
                acc[unit][j % 2][c],
                kw[pl.ds(base + j * TQ + c * PIECE, PIECE), :],
                load_staged_rhs=staged,
            )

        def keep(h, unit, j, c, top):
            part = pltpu.matmul_pop(acc[unit][j % 2][c])
            if j == TILES - 1:
                part = part + corner[c * PIECE : (c + 1) * PIECE, :]
            start = j * TQ + c * PIECE
            scores[h % SLOTS, start : start + PIECE, :] = part
            most = jnp.max(part.reshape(PIECE // 8, 8, TQ), axis=0)
            return most if top is None else jnp.maximum(top, most)

        def weigh(h, unit, j, c, top):
            start = j * TQ + c * PIECE
            part = jnp.exp2((scores[h % SLOTS, start : start + PIECE, :] - top) * SCALE)
            weights[unit, j % 2, c * PIECE : (c + 1) * PIECE, :] = part.astype(jnp.bfloat16)

        def gather(unit, j, at, slot):
            pltpu.matmul_push_rhs(weights[unit, j % 2], 1, unit)
            pltpu.matmul_acc_lhs(
                total[unit],
                vt[slot, :, pl.ds(pl.multiple_of(at + j * TQ, TQ), TQ)],
                load_staged_rhs=1,
            )

        def put(h, unit, out):
            sums = pltpu.matmul_pop(total[unit])
            rows = (sums[:HEAD_SIZE] / sums[HEAD_SIZE : HEAD_SIZE + 1]).T
            outs[out, :, columns(h)] = rows.astype(jnp.bfloat16)

        def step(ahead, behind, unit, top, at, slot, out):
            most = None
            if behind is not None:
                top = jnp.broadcast_to(jnp.max(top, axis=0, keepdims=True), (8, TQ))
                top = jnp.concatenate([top] * (PIECE // 8), axis=0)
            for i in range(TILES * PIECES + PIECES):
                j, c = divmod(i, PIECES)
                if ahead is not None and i < TILES * PIECES:
                    score(ahead, unit, j, c)
                if ahead is not None and 1 <= i <= TILES * PIECES:
                    most = keep(ahead, unit, *divmod(i - 1, PIECES), most)
                if behind is not None and i < TILES * PIECES:
                    weigh(behind, 1 - unit, j, c, top)
                    if c == PIECES - 1:
                        gather(1 - unit, j, at, slot)
            if behind is not None:
                put(behind, 1 - unit, out)
            return most

        last = s - 1 + 3
        old = (
            pl.multiple_of(lax.rem(last + 1, 2) * TQ, TQ),
            lax.rem((last + 1) // 2, 2),
            lax.rem(last, 3),
        )
        new = (base, lax.rem(g, 2), lax.rem(s, 3))

        @pl.when(s < STEPS)
        def _():
            found = {h - GROUP: tops[h - GROUP + LAG] for h in range(GROUP - LAG, GROUP)}
            for h in range(GROUP):
                behind = h - LAG
                where = old if behind < 0 else new
                found[h] = step(h, behind % GROUP, h % 2, found[behind], *where)
            for h in range(GROUP - LAG, GROUP):
                tops[h - GROUP + LAG] = found[h]

        @pl.when(s == STEPS)
        def _():
            for h in range(LAG):
                step(None, GROUP - LAG + h, h % 2, tops[h], *old)

    pl.run_scoped(
        work,
        [
            [[pltpu.ACC(u)((PIECE, TQ), jnp.float32) for _ in range(PIECES)] for _ in range(2)]
            for u in range(2)
        ],
        [pltpu.ACC(u)((HEAD_SIZE + 16, TQ), jnp.float32) for u in range(2)],
    )

    @pl.when(s >= 1)
    def _():
        result(s - 1).start()

    @pl.when(s == STEPS)
    def _():
        def finish(h, carry):
            for copy in (*far(h), *near(h)):
                copy.wait_send()
            return carry

        lax.fori_loop(0, KEY_HEADS, finish, 0)
        result(s - 2).wait()
        result(s - 1).wait()


def attend(q_extra, k_extra, queries, keys, values):
    def head(s):
        return jnp.minimum(s // 2, KEY_HEADS - 1)

    def own(s):
        return (0, 0, head(s))

    return pl.pallas_call(
        kernel,
        grid=(STEPS + 1,),
        in_specs=[
            pl.BlockSpec((1, TQ, WIDTH), lambda s: (0, lax.rem(s, 2), head(s))),
            pl.BlockSpec((TQ, HEAD_SIZE), lambda s: (lax.rem(s, 2), 0)),
            pl.BlockSpec((1, ROWS, HEAD_SIZE), own),
            pl.BlockSpec((1, ROWS, HEAD_SIZE), own),
            pl.BlockSpec(memory_space=pltpu.HBM),
            pl.BlockSpec(memory_space=pltpu.HBM),
            pl.BlockSpec((3 * ROWS, HEAD_SIZE), lambda s: (0, 0)),
        ],
        out_specs=pl.BlockSpec(memory_space=pltpu.HBM),
        scratch_shapes=[
            *[pltpu.VMEM((KEY_HEADS, ROWS, HEAD_SIZE), jnp.bfloat16)] * 4,
            pltpu.VMEM((3 * ROWS, 2 * HEAD_SIZE), jnp.bfloat16),
            pltpu.VMEM((2, HEAD_SIZE + 16, 3 * ROWS), jnp.bfloat16),
            pltpu.VMEM((TQ, TQ), jnp.float32),
            pltpu.VMEM((SLOTS, SPAN, TQ), jnp.float32),
            pltpu.VMEM((2, 2, TQ, TQ), jnp.bfloat16),
            pltpu.VMEM((LAG, 8, TQ), jnp.float32),
            pltpu.VMEM((3, TQ, WIDTH), jnp.bfloat16),
            pltpu.SemaphoreType.DMA((4, KEY_HEADS)),
            pltpu.SemaphoreType.DMA((4, KEY_HEADS)),
            pltpu.SemaphoreType.DMA((3,)),
        ],
        out_shape=jax.ShapeDtypeStruct((1, ROWS, HQ * HEAD_SIZE), jnp.bfloat16),
        compiler_params=pltpu.CompilerParams(
            vmem_limit_bytes=50 << 20, collective_id=0, has_side_effects=True
        ),
    )(queries, q_extra, keys, values, keys, values, k_extra)


def on_device(queries, keys, values, doc_lengths):
    rep = lax.axis_index("rep")
    ctx = lax.axis_index("ctx")
    lengths = lax.dynamic_index_in_dim(doc_lengths, rep, 0, keepdims=False)
    documents = lengths.shape[0]
    order = jnp.arange(documents)
    ends = jnp.sum(jnp.where(order[None, :] <= order[:, None], lengths[None, :], 0), axis=1)
    positions = (ctx - 2) * ROWS + jnp.arange(3 * ROWS, dtype=jnp.int32)
    segment = jnp.sum((positions[:, None] >= ends[None, :]).astype(jnp.int32), axis=1)
    segment = jnp.where(positions < 0, documents, segment)
    same = segment[:, None] == jnp.arange(HEAD_SIZE, dtype=jnp.int32)[None, :]
    k_extra = same.astype(jnp.bfloat16)
    q_extra = jnp.where(same[2 * ROWS :], 0.0, FAR_BELOW).astype(jnp.bfloat16)
    return attend(q_extra, k_extra, queries, keys, values)


def solution(mesh):
    return jax.shard_map(
        on_device,
        mesh=mesh,
        in_specs=(P("rep", "ctx", None), P("rep", "ctx", None), P("rep", "ctx", None), P()),
        out_specs=P("rep", "ctx", None),
        check_vma=False,
    )
```

```python
import math

import jax
import jax.numpy as jnp
from jax import lax
from jax.experimental import pallas as pl
from jax.experimental.pallas import tpu as pltpu
from jax.sharding import PartitionSpec as P

MESH = pl.DeviceIdType.MESH
HQ = 64
KEY_HEADS = 8
HEAD_SIZE = 128
GROUP = 8
WIDTH = GROUP * HEAD_SIZE
ROWS = 512
TQ = 256
SPAN = 1280
SCALE = math.log2(math.e) / math.sqrt(HEAD_SIZE)
AHEAD = 3
PIECE = 128
PIECES = TQ // PIECE
TILES = SPAN // TQ
SLOTS = 4
LAG = 3
STEPS = 2 * KEY_HEADS
FAR_BELOW = -131072.0


def kernel(
    q_ref, q_extra, own_k, own_v, all_k, all_v, k_extra, o_ref,
    far_k, far_v, near_k, near_v, kw, vt, corner, scores, tops, outs, send, recv, sent,
):
    s = pl.program_id(0)
    g = s // 2
    t = lax.rem(s, 2)
    ctx = lax.axis_index("ctx")
    n = lax.axis_size("ctx")
    odd = lax.rem(ctx, 2)
    after = lax.rem(ctx + 2, n)
    before = lax.rem(ctx + n - 2, n)
    beside = ctx + 1 - 2 * odd

    def move(kind, h, source, target, device):
        return pltpu.make_async_remote_copy(
            src_ref=source,
            dst_ref=target.at[h],
            send_sem=send.at[kind, h],
            recv_sem=recv.at[kind, h],
            device_id={"ctx": device},
            device_id_type=MESH,
        )

    def own(ref, h):
        return ref.at[0, :, pl.ds(pl.multiple_of(h * HEAD_SIZE, HEAD_SIZE), HEAD_SIZE)]

    def far(h):
        return (
            move(0, h, own(all_k, h), far_k, after),
            move(1, h, own(all_v, h), far_v, after),
        )

    def near(h):
        return (
            move(2, h, own(all_k, h), near_k, beside),
            move(3, h, own(all_v, h), near_v, beside),
        )

    def relay(h):
        return (
            move(2, h, far_k.at[h], near_k, beside),
            move(3, h, far_v.at[h], near_v, beside),
        )

    def issue(h):
        for copy in far(h):
            copy.start()

        @pl.when(odd == 0)
        def _():
            for copy in near(h):
                copy.start()

    def forward(h):
        for copy in far(h):
            copy.wait_recv()

        @pl.when(odd == 1)
        def _():
            for copy in relay(h):
                copy.start()

    def result(step):
        row = pl.multiple_of(lax.rem(step, 2) * TQ, TQ)
        column = pl.multiple_of(step // 2 * WIDTH, WIDTH)
        slot = lax.rem(step, 3)
        return pltpu.make_async_copy(
            outs.at[slot],
            o_ref.at[0, pl.ds(row, TQ), pl.ds(column, WIDTH)],
            sent.at[slot],
        )

    @pl.when(s == 0)
    def _():
        barrier = pltpu.get_barrier_semaphore()
        for device in (after, before, beside):
            pl.semaphore_signal(barrier, inc=1, device_id={"ctx": device}, device_id_type=MESH)
        pl.semaphore_wait(barrier, 3)
        lax.fori_loop(0, AHEAD, lambda h, c: (issue(h), c)[1], 0)
        kw[:, HEAD_SIZE:] = k_extra[...]
        for i in range(2):
            vt[i, HEAD_SIZE:, :] = jnp.ones((16, 3 * ROWS), jnp.bfloat16)
        below = lax.broadcasted_iota(jnp.int32, (TQ, TQ), 0)
        across = lax.broadcasted_iota(jnp.int32, (TQ, TQ), 1)
        corner[...] = jnp.where(below <= across, 0.0, FAR_BELOW)
        scores[SLOTS - LAG :] = jnp.zeros((LAG, SPAN, TQ), jnp.float32)
        tops[...] = jnp.zeros_like(tops)
        forward(0)

    @pl.when((t == 0) & (g < KEY_HEADS))
    def _():
        @pl.when(g + AHEAD < KEY_HEADS)
        def _():
            issue(g + AHEAD)

        for copy in near(g):
            copy.wait_recv()
        slot = lax.rem(g, 2)
        for i, (key, value) in enumerate(
            ((far_k[g], far_v[g]), (near_k[g], near_v[g]), (own_k[0], own_v[0]))
        ):
            kw[i * ROWS : (i + 1) * ROWS, :HEAD_SIZE] = key
            vt[slot, :HEAD_SIZE, i * ROWS : (i + 1) * ROWS] = value.T

    @pl.when((t == 1) & (g + 1 < KEY_HEADS))
    def _():
        forward(g + 1)

    @pl.when(s >= 3)
    def _():
        result(s - 3).wait()

    def work(acc, total):
        def columns(h):
            return slice(h * HEAD_SIZE, (h + 1) * HEAD_SIZE)

        base = pl.multiple_of(t * TQ, TQ)

        def score(h, unit, j, c):
            staged = None
            if j == 0 and c == 0:
                staged = 0
                query = jnp.concatenate([q_ref[0, :, columns(h)], q_extra[...]], axis=1)
                pltpu.matmul_push_rhs(query, 0, unit, transpose=True)
            pltpu.matmul_acc_lhs(
                acc[unit][j % 2][c],
                kw[pl.ds(base + j * TQ + c * PIECE, PIECE), :],
                load_staged_rhs=staged,
            )

        def keep(h, unit, j, c, top):
            part = pltpu.matmul_pop(acc[unit][j % 2][c])
            if j == TILES - 1:
                part = part + corner[c * PIECE : (c + 1) * PIECE, :]
            start = j * TQ + c * PIECE
            scores[h % SLOTS, start : start + PIECE, :] = part
            most = jnp.max(part.reshape(PIECE // 8, 8, TQ), axis=0)
            return most if top is None else jnp.maximum(top, most)

        def weigh(h, unit, j, c, top):
            start = j * TQ + c * PIECE
            part = jnp.exp2((scores[h % SLOTS, start : start + PIECE, :] - top) * SCALE)
            return part.astype(jnp.bfloat16)

        def gather(unit, j, at, slot, parts):
            pltpu.matmul_push_rhs(jnp.concatenate(parts, axis=0), 1, unit)
            pltpu.matmul_acc_lhs(
                total[unit],
                vt[slot, :, pl.ds(pl.multiple_of(at + j * TQ, TQ), TQ)],
                load_staged_rhs=1,
            )

        def put(h, unit, out):
            sums = pltpu.matmul_pop(total[unit])
            rows = (sums[:HEAD_SIZE] / sums[HEAD_SIZE : HEAD_SIZE + 1]).T
            outs[out, :, columns(h)] = rows.astype(jnp.bfloat16)

        def step(ahead, behind, unit, top, at, slot, out):
            most = None
            if behind is not None:
                top = jnp.broadcast_to(jnp.max(top, axis=0, keepdims=True), (8, TQ))
                top = jnp.concatenate([top] * (PIECE // 8), axis=0)
            for i in range(TILES * PIECES + PIECES):
                j, c = divmod(i, PIECES)
                if ahead is not None and i < TILES * PIECES:
                    score(ahead, unit, j, c)
                if ahead is not None and 1 <= i <= TILES * PIECES:
                    most = keep(ahead, unit, *divmod(i - 1, PIECES), most)
                if behind is not None and i < TILES * PIECES:
                    parts = [] if c == 0 else parts
                    parts.append(weigh(behind, 1 - unit, j, c, top))
                    if c == PIECES - 1:
                        gather(1 - unit, j, at, slot, parts)
            if behind is not None:
                put(behind, 1 - unit, out)
            return most

        last = s - 1 + 3
        old = (
            pl.multiple_of(lax.rem(last + 1, 2) * TQ, TQ),
            lax.rem((last + 1) // 2, 2),
            lax.rem(last, 3),
        )
        new = (base, lax.rem(g, 2), lax.rem(s, 3))

        @pl.when(s < STEPS)
        def _():
            found = {h - GROUP: tops[h - GROUP + LAG] for h in range(GROUP - LAG, GROUP)}
            for h in range(GROUP):
                behind = h - LAG
                where = old if behind < 0 else new
                found[h] = step(h, behind % GROUP, h % 2, found[behind], *where)
            for h in range(GROUP - LAG, GROUP):
                tops[h - GROUP + LAG] = found[h]

        @pl.when(s == STEPS)
        def _():
            for h in range(LAG):
                step(None, GROUP - LAG + h, h % 2, tops[h], *old)

    pl.run_scoped(
        work,
        [
            [[pltpu.ACC(u)((PIECE, TQ), jnp.float32) for _ in range(PIECES)] for _ in range(2)]
            for u in range(2)
        ],
        [pltpu.ACC(u)((HEAD_SIZE + 16, TQ), jnp.float32) for u in range(2)],
    )

    @pl.when(s >= 1)
    def _():
        result(s - 1).start()

    @pl.when(s == STEPS)
    def _():
        def finish(h, carry):
            for copy in (*far(h), *near(h)):
                copy.wait_send()
            return carry

        lax.fori_loop(0, KEY_HEADS, finish, 0)
        result(s - 2).wait()
        result(s - 1).wait()


def attend(q_extra, k_extra, queries, keys, values):
    def head(s):
        return jnp.minimum(s // 2, KEY_HEADS - 1)

    def own(s):
        return (0, 0, head(s))

    return pl.pallas_call(
        kernel,
        grid=(STEPS + 1,),
        in_specs=[
            pl.BlockSpec((1, TQ, WIDTH), lambda s: (0, lax.rem(s, 2), head(s))),
            pl.BlockSpec((TQ, HEAD_SIZE), lambda s: (lax.rem(s, 2), 0)),
            pl.BlockSpec((1, ROWS, HEAD_SIZE), own),
            pl.BlockSpec((1, ROWS, HEAD_SIZE), own),
            pl.BlockSpec(memory_space=pltpu.HBM),
            pl.BlockSpec(memory_space=pltpu.HBM),
            pl.BlockSpec((3 * ROWS, HEAD_SIZE), lambda s: (0, 0)),
        ],
        out_specs=pl.BlockSpec(memory_space=pltpu.HBM),
        scratch_shapes=[
            *[pltpu.VMEM((KEY_HEADS, ROWS, HEAD_SIZE), jnp.bfloat16)] * 4,
            pltpu.VMEM((3 * ROWS, 2 * HEAD_SIZE), jnp.bfloat16),
            pltpu.VMEM((2, HEAD_SIZE + 16, 3 * ROWS), jnp.bfloat16),
            pltpu.VMEM((TQ, TQ), jnp.float32),
            pltpu.VMEM((SLOTS, SPAN, TQ), jnp.float32),
            pltpu.VMEM((LAG, 8, TQ), jnp.float32),
            pltpu.VMEM((3, TQ, WIDTH), jnp.bfloat16),
            pltpu.SemaphoreType.DMA((4, KEY_HEADS)),
            pltpu.SemaphoreType.DMA((4, KEY_HEADS)),
            pltpu.SemaphoreType.DMA((3,)),
        ],
        out_shape=jax.ShapeDtypeStruct((1, ROWS, HQ * HEAD_SIZE), jnp.bfloat16),
        compiler_params=pltpu.CompilerParams(
            vmem_limit_bytes=63 << 20, collective_id=0, has_side_effects=True
        ),
    )(queries, q_extra, keys, values, keys, values, k_extra)


def on_device(queries, keys, values, doc_lengths):
    rep = lax.axis_index("rep")
    ctx = lax.axis_index("ctx")
    lengths = lax.dynamic_index_in_dim(doc_lengths, rep, 0, keepdims=False)
    documents = lengths.shape[0]
    order = jnp.arange(documents)
    ends = jnp.sum(jnp.where(order[None, :] <= order[:, None], lengths[None, :], 0), axis=1)
    positions = (ctx - 2) * ROWS + jnp.arange(3 * ROWS, dtype=jnp.int32)
    segment = jnp.sum((positions[:, None] >= ends[None, :]).astype(jnp.int32), axis=1)
    segment = jnp.where(positions < 0, documents, segment)
    same = segment[:, None] == jnp.arange(HEAD_SIZE, dtype=jnp.int32)[None, :]
    k_extra = same.astype(jnp.bfloat16)
    q_extra = jnp.where(same[2 * ROWS :], 0.0, FAR_BELOW).astype(jnp.bfloat16)
    return attend(q_extra, k_extra, queries, keys, values)


def solution(mesh):
    return jax.shard_map(
        on_device,
        mesh=mesh,
        in_specs=(P("rep", "ctx", None), P("rep", "ctx", None), P("rep", "ctx", None), P()),
        out_specs=P("rep", "ctx", None),
        check_vma=False,
    )
```

```python
import math

import jax
import jax.numpy as jnp
from jax import lax
from jax.experimental import pallas as pl
from jax.experimental.pallas import tpu as pltpu
from jax.sharding import PartitionSpec as P

MESH = pl.DeviceIdType.MESH
HQ = 64
KEY_HEADS = 8
HEAD_SIZE = 128
GROUP = 8
WIDTH = GROUP * HEAD_SIZE
ROWS = 512
TQ = 256
SPAN = 1280
SCALE = math.log2(math.e) / math.sqrt(HEAD_SIZE)
AHEAD = 3
PIECE = 128
PIECES = TQ // PIECE
TILES = SPAN // TQ
SLOTS = 4
LAG = 3
STEPS = 2 * KEY_HEADS
FAR_BELOW = -131072.0


def kernel(
    q_ref, bounds, own_k, own_v, all_k, all_v, o_ref,
    far_k, far_v, near_k, near_v, kw, vt, q_extra, corner, scores, tops, outs, send, recv, sent,
):
    s = pl.program_id(0)
    g = s // 2
    t = lax.rem(s, 2)
    ctx = lax.axis_index("ctx")
    n = lax.axis_size("ctx")
    odd = lax.rem(ctx, 2)
    after = lax.rem(ctx + 2, n)
    before = lax.rem(ctx + n - 2, n)
    beside = ctx + 1 - 2 * odd

    def move(kind, h, source, target, device):
        return pltpu.make_async_remote_copy(
            src_ref=source,
            dst_ref=target.at[h],
            send_sem=send.at[kind, h],
            recv_sem=recv.at[kind, h],
            device_id={"ctx": device},
            device_id_type=MESH,
        )

    def own(ref, h):
        return ref.at[0, :, pl.ds(pl.multiple_of(h * HEAD_SIZE, HEAD_SIZE), HEAD_SIZE)]

    def far(h):
        return (
            move(0, h, own(all_k, h), far_k, after),
            move(1, h, own(all_v, h), far_v, after),
        )

    def near(h):
        return (
            move(2, h, own(all_k, h), near_k, beside),
            move(3, h, own(all_v, h), near_v, beside),
        )

    def relay(h):
        return (
            move(2, h, far_k.at[h], near_k, beside),
            move(3, h, far_v.at[h], near_v, beside),
        )

    def issue(h):
        for copy in far(h):
            copy.start()

        @pl.when(odd == 0)
        def _():
            for copy in near(h):
                copy.start()

    def forward(h):
        for copy in far(h):
            copy.wait_recv()

        @pl.when(odd == 1)
        def _():
            for copy in relay(h):
                copy.start()

    def result(step):
        row = pl.multiple_of(lax.rem(step, 2) * TQ, TQ)
        column = pl.multiple_of(step // 2 * WIDTH, WIDTH)
        slot = lax.rem(step, 3)
        return pltpu.make_async_copy(
            outs.at[slot],
            o_ref.at[0, pl.ds(row, TQ), pl.ds(column, WIDTH)],
            sent.at[slot],
        )

    @pl.when(s == 0)
    def _():
        barrier = pltpu.get_barrier_semaphore()
        for device in (after, before, beside):
            pl.semaphore_signal(barrier, inc=1, device_id={"ctx": device}, device_id_type=MESH)
        pl.semaphore_wait(barrier, 3)
        lax.fori_loop(0, AHEAD, lambda h, c: (issue(h), c)[1], 0)
        place = lax.broadcasted_iota(jnp.int32, (3 * ROWS, HEAD_SIZE), 0) + (ctx - 2) * ROWS
        same = (place >= bounds[0:1, :]) & (place < bounds[1:2, :])
        kw[:, HEAD_SIZE:] = jnp.where(same, 1.0, 0.0).astype(jnp.bfloat16)
        place = lax.broadcasted_iota(jnp.int32, (ROWS, HEAD_SIZE), 0) + ctx * ROWS
        same = (place >= bounds[0:1, :]) & (place < bounds[1:2, :])
        q_extra[...] = jnp.where(same, 0.0, FAR_BELOW).astype(jnp.bfloat16)
        for i in range(2):
            vt[i, HEAD_SIZE:, :] = jnp.ones((16, 3 * ROWS), jnp.bfloat16)
        below = lax.broadcasted_iota(jnp.int32, (TQ, TQ), 0)
        across = lax.broadcasted_iota(jnp.int32, (TQ, TQ), 1)
        corner[...] = jnp.where(below <= across, 0.0, FAR_BELOW)
        scores[SLOTS - LAG :] = jnp.zeros((LAG, SPAN, TQ), jnp.float32)
        tops[...] = jnp.zeros_like(tops)
        forward(0)

    @pl.when((t == 0) & (g < KEY_HEADS))
    def _():
        @pl.when(g + AHEAD < KEY_HEADS)
        def _():
            issue(g + AHEAD)

        for copy in near(g):
            copy.wait_recv()
        slot = lax.rem(g, 2)
        for i, (key, value) in enumerate(
            ((far_k[g], far_v[g]), (near_k[g], near_v[g]), (own_k[0], own_v[0]))
        ):
            kw[i * ROWS : (i + 1) * ROWS, :HEAD_SIZE] = key
            vt[slot, :HEAD_SIZE, i * ROWS : (i + 1) * ROWS] = value.T

    @pl.when((t == 1) & (g + 1 < KEY_HEADS))
    def _():
        forward(g + 1)

    @pl.when(s >= 3)
    def _():
        result(s - 3).wait()

    def work(acc, total):
        def columns(h):
            return slice(h * HEAD_SIZE, (h + 1) * HEAD_SIZE)

        base = pl.multiple_of(t * TQ, TQ)
        extra = q_extra[pl.ds(base, TQ), :]

        def score(h, unit, j, c):
            staged = None
            if j == 0 and c == 0:
                staged = 0
                query = jnp.concatenate([q_ref[0, :, columns(h)], extra], axis=1)
                pltpu.matmul_push_rhs(query, 0, unit, transpose=True)
            pltpu.matmul_acc_lhs(
                acc[unit][j % 2][c],
                kw[pl.ds(base + j * TQ + c * PIECE, PIECE), :],
                load_staged_rhs=staged,
            )

        def keep(h, unit, j, c, top):
            part = pltpu.matmul_pop(acc[unit][j % 2][c])
            if j == TILES - 1:
                part = part + corner[c * PIECE : (c + 1) * PIECE, :]
            start = j * TQ + c * PIECE
            scores[h % SLOTS, start : start + PIECE, :] = part
            most = jnp.max(part.reshape(PIECE // 8, 8, TQ), axis=0)
            return most if top is None else jnp.maximum(top, most)

        def weigh(h, unit, j, c, top):
            start = j * TQ + c * PIECE
            part = jnp.exp2((scores[h % SLOTS, start : start + PIECE, :] - top) * SCALE)
            return part.astype(jnp.bfloat16)

        def gather(unit, j, at, slot, parts):
            pltpu.matmul_push_rhs(jnp.concatenate(parts, axis=0), 1, unit)
            pltpu.matmul_acc_lhs(
                total[unit],
                vt[slot, :, pl.ds(pl.multiple_of(at + j * TQ, TQ), TQ)],
                load_staged_rhs=1,
            )

        def put(h, unit, out):
            sums = pltpu.matmul_pop(total[unit])
            rows = (sums[:HEAD_SIZE] / sums[HEAD_SIZE : HEAD_SIZE + 1]).T
            outs[out, :, columns(h)] = rows.astype(jnp.bfloat16)

        def step(ahead, behind, unit, top, at, slot, out):
            most = None
            if behind is not None:
                top = jnp.broadcast_to(jnp.max(top, axis=0, keepdims=True), (8, TQ))
                top = jnp.concatenate([top] * (PIECE // 8), axis=0)
            for i in range(TILES * PIECES + PIECES):
                j, c = divmod(i, PIECES)
                if ahead is not None and i < TILES * PIECES:
                    score(ahead, unit, j, c)
                if ahead is not None and 1 <= i <= TILES * PIECES:
                    most = keep(ahead, unit, *divmod(i - 1, PIECES), most)
                if behind is not None and i < TILES * PIECES:
                    parts = [] if c == 0 else parts
                    parts.append(weigh(behind, 1 - unit, j, c, top))
                    if c == PIECES - 1:
                        gather(1 - unit, j, at, slot, parts)
            if behind is not None:
                put(behind, 1 - unit, out)
            return most

        last = s - 1 + 3
        old = (
            pl.multiple_of(lax.rem(last + 1, 2) * TQ, TQ),
            lax.rem((last + 1) // 2, 2),
            lax.rem(last, 3),
        )
        new = (base, lax.rem(g, 2), lax.rem(s, 3))

        @pl.when(s < STEPS)
        def _():
            found = {h - GROUP: tops[h - GROUP + LAG] for h in range(GROUP - LAG, GROUP)}
            for h in range(GROUP):
                behind = h - LAG
                where = old if behind < 0 else new
                found[h] = step(h, behind % GROUP, h % 2, found[behind], *where)
            for h in range(GROUP - LAG, GROUP):
                tops[h - GROUP + LAG] = found[h]

        @pl.when(s == STEPS)
        def _():
            for h in range(LAG):
                step(None, GROUP - LAG + h, h % 2, tops[h], *old)

    pl.run_scoped(
        work,
        [
            [[pltpu.ACC(u)((PIECE, TQ), jnp.float32) for _ in range(PIECES)] for _ in range(2)]
            for u in range(2)
        ],
        [pltpu.ACC(u)((HEAD_SIZE + 16, TQ), jnp.float32) for u in range(2)],
    )

    @pl.when(s >= 1)
    def _():
        result(s - 1).start()

    @pl.when(s == STEPS)
    def _():
        def finish(h, carry):
            for copy in (*far(h), *near(h)):
                copy.wait_send()
            return carry

        lax.fori_loop(0, KEY_HEADS, finish, 0)
        result(s - 2).wait()
        result(s - 1).wait()


def attend(bounds, queries, keys, values):
    def head(s):
        return jnp.minimum(s // 2, KEY_HEADS - 1)

    def own(s):
        return (0, 0, head(s))

    return pl.pallas_call(
        kernel,
        grid=(STEPS + 1,),
        in_specs=[
            pl.BlockSpec((1, TQ, WIDTH), lambda s: (0, lax.rem(s, 2), head(s))),
            pl.BlockSpec((8, HEAD_SIZE), lambda s: (0, 0)),
            pl.BlockSpec((1, ROWS, HEAD_SIZE), own),
            pl.BlockSpec((1, ROWS, HEAD_SIZE), own),
            pl.BlockSpec(memory_space=pltpu.HBM),
            pl.BlockSpec(memory_space=pltpu.HBM),
        ],
        out_specs=pl.BlockSpec(memory_space=pltpu.HBM),
        scratch_shapes=[
            *[pltpu.VMEM((KEY_HEADS, ROWS, HEAD_SIZE), jnp.bfloat16)] * 4,
            pltpu.VMEM((3 * ROWS, 2 * HEAD_SIZE), jnp.bfloat16),
            pltpu.VMEM((2, HEAD_SIZE + 16, 3 * ROWS), jnp.bfloat16),
            pltpu.VMEM((ROWS, HEAD_SIZE), jnp.bfloat16),
            pltpu.VMEM((TQ, TQ), jnp.float32),
            pltpu.VMEM((SLOTS, SPAN, TQ), jnp.float32),
            pltpu.VMEM((LAG, 8, TQ), jnp.float32),
            pltpu.VMEM((3, TQ, WIDTH), jnp.bfloat16),
            pltpu.SemaphoreType.DMA((4, KEY_HEADS)),
            pltpu.SemaphoreType.DMA((4, KEY_HEADS)),
            pltpu.SemaphoreType.DMA((3,)),
        ],
        out_shape=jax.ShapeDtypeStruct((1, ROWS, HQ * HEAD_SIZE), jnp.bfloat16),
        compiler_params=pltpu.CompilerParams(
            vmem_limit_bytes=63 << 20, collective_id=0, has_side_effects=True
        ),
    )(queries, bounds, keys, values, keys, values)


def on_device(queries, keys, values, doc_lengths):
    rep = lax.axis_index("rep")
    lengths = lax.dynamic_index_in_dim(doc_lengths, rep, 0, keepdims=False)
    documents = lengths.shape[0]
    order = jnp.arange(documents)[None, :]
    lane = jnp.arange(HEAD_SIZE)[:, None]
    starts = jnp.sum(jnp.where(order < lane, lengths[None, :], 0), axis=1)
    ends = jnp.sum(jnp.where(order <= lane, lengths[None, :], 0), axis=1)
    outside = lane[:, 0] == documents
    starts = jnp.where(outside, -(1 << 20), starts)
    ends = jnp.where(outside, 0, ends)
    bounds = jnp.broadcast_to(jnp.stack([starts, ends])[None], (4, 2, HEAD_SIZE))
    bounds = bounds.reshape(8, HEAD_SIZE).astype(jnp.int32)
    return attend(bounds, queries, keys, values)


def solution(mesh):
    return jax.shard_map(
        on_device,
        mesh=mesh,
        in_specs=(P("rep", "ctx", None), P("rep", "ctx", None), P("rep", "ctx", None), P()),
        out_specs=P("rep", "ctx", None),
        check_vma=False,
    )
```
